512 devices in a mesh: seq: 128 (over x, y, z_hi, core), user: 4 (over z_lo).
Axes of the slice: x: 4, y: 4, z: 16 (z_hi: 4, z_lo: 4; z = z_hi * 4 + z_lo), core: 2. Of those that a mesh axis runs over, the one named last changes fastest.
Arguments:
- inputs: bfloat16 [4, 131072, 256], P('user', 'seq'), may hold values from -6 to 6
- kernel_weight_first: bfloat16 [3, 256, 256], replicated, may hold values from -0.21875 to 0.21875
- norm_gain_first: float32 [256], replicated, may hold values from 0.1 to 1.9
- norm_bias_first: float32 [256], replicated, may hold values from -0.5 to 0.5
- kernel_weight_second: bfloat16 [3, 256, 256], replicated, may hold values from -0.21875 to 0.21875
- norm_gain_second: float32 [256], replicated, may hold values from 0.1 to 1.9
- norm_bias_second: float32 [256], replicated, may hold values from -0.5 to 0.5
- cotangent: bfloat16 [4, 131072, 256], P('user', 'seq'), may hold values from -9 to 9
Outputs:
- grad_inputs: bfloat16 [4, 131072, 256], P('user', 'seq')
- grad_weight_one: float32 [3, 256, 256], replicated
- grad_gain_one: float32 [256], replicated
- grad_bias_one: float32 [256], replicated
- grad_weight_two: float32 [3, 256, 256], replicated
- grad_gain_two: float32 [256], replicated
- grad_bias_two: float32 [256], replicated
The draws below stay inside these ranges and needn't reach their ends.
All inputs are finite; a program needn't handle non-finite values.
Results may differ from the reference program's by a relative error of at most 0.012.
Values may be sent and summed in bfloat16 or wider, within the bound.
A program may use at most 64 MiB of HBM per device.

```python
import jax
import jax.numpy as jnp
from jax import lax

C = 256
DILATION_FIRST1 = 1024
DILATION_SECOND2 = 2048
SEQ = 131072
USERS = 4


def draw_cotangent(key, part):
    key = jax.random.fold_in(key, 7)
    ramp = 0.5 + jnp.arange(SEQ, dtype=jnp.float32) / SEQ
    base = jnp.clip(jax.random.normal(key, (USERS, SEQ, C), jnp.float32), -6.0, 6.0)
    return (base * ramp[None, :, None]).astype(jnp.bfloat16)


def levels(own_key, shape, pieces, smallest, high):
    level, own = 1.0, jax.random.fold_in(own_key, 6)
    for axis_at, shards_of in pieces:
        heights = jnp.exp(jax.random.uniform(jax.random.fold_in(own, axis_at), (shards_of,), jnp.float32, smallest / len(pieces), high / len(pieces)))
        level = level * jnp.repeat(heights, shape[axis_at] // shards_of).reshape([-1 if axis == axis_at else 1 for axis in range(len(shape))])
    return level


def normal_values(rng, shape, width, bound, pieces=(), kind=jnp.bfloat16):
    factor_of = levels(rng, shape, pieces, -0.22, 0.18) if pieces else 1.0
    values = jax.random.normal(rng, shape, jnp.float32) * width * factor_of
    return jnp.minimum(jnp.maximum(values, -bound), bound).astype(kind)


def setup_inputs(seed: int = 0) -> dict:
    key_list = jax.random.split(jax.random.key(seed), 9)
    return {
        "inputs": normal_values(key_list[0], (USERS, SEQ, C), 1.0, 6.0, ((0, 4), (1, 128))),
        "kernel_weight_first": normal_values(key_list[1], (3, C, C), (3 * C) ** -0.5, 0.21875),
        "norm_gain_first": jnp.clip(1.0 + 0.18 * jax.random.normal(key_list[2], (C,), jnp.float32), 0.1, 1.9),
        "norm_bias_first": jnp.clip(jax.random.uniform(key_list[3], (C,), jnp.float32, -0.5, 0.5), -0.5, 0.5),
        "kernel_weight_second": normal_values(key_list[4], (3, C, C), (3 * C) ** -0.5, 0.21875),
        "norm_gain_second": jnp.clip(1.0 + 0.18 * jax.random.normal(key_list[5], (C,), jnp.float32), 0.1, 1.9),
        "norm_bias_second": jnp.clip(jax.random.uniform(key_list[6], (C,), jnp.float32, -0.5, 0.5), -0.5, 0.5),
        "cotangent": draw_cotangent(jax.random.fold_in(key_list[8], 71), 0),
    }


EPSILON = 1e-05

def activate(values):
    return values * jax.nn.sigmoid(values)

def activate_slope(values):
    sigma = jax.nn.sigmoid(values)
    return sigma * (1.0 + values * (1.0 - sigma))

def shift_past(rows, offset):
    filler = jnp.zeros((offset, rows.shape[1]), rows.dtype)
    return jnp.concatenate([filler, rows[:rows.shape[0] - offset]], axis=0)

def shift_future(rows, offset):
    filler = jnp.zeros((offset, rows.shape[1]), rows.dtype)
    return jnp.concatenate([rows[offset:], filler], axis=0)

def normalize(pre):
    center = lax.optimization_barrier(jnp.mean(pre, axis=-1, keepdims=True))
    spread = lax.optimization_barrier(jnp.mean(jnp.square(pre - center), axis=-1, keepdims=True))
    inverse = lax.rsqrt(spread + EPSILON)
    return ((pre - center) * inverse, inverse)

def residual_layer_forward(source_rows, weight, gain, bias, dilation):
    shifted = [source_rows, shift_past(source_rows, dilation), shift_past(source_rows, 2 * dilation)]
    pre = jnp.dot(shifted[0], weight[0], preferred_element_type=jnp.float32)
    for offset in range(1, 3):
        pre = pre + jnp.dot(shifted[offset], weight[offset], preferred_element_type=jnp.float32)
    normed, inverse = normalize(pre)
    active = normed * gain + bias
    return (shifted, normed, inverse, active)

def residual_layer_backward(g_out, shifted, normed, inverse, active, weight, gain, dilation):
    g_act = g_out * activate_slope(active)
    gain_sum = lax.optimization_barrier(jnp.sum(g_act * normed, axis=0))
    bias_sum = lax.optimization_barrier(jnp.sum(g_act, axis=0))
    g_norm = g_act * gain
    g_pre = inverse * (g_norm - lax.optimization_barrier(jnp.mean(g_norm, axis=-1, keepdims=True)) - normed * lax.optimization_barrier(jnp.mean(g_norm * normed, axis=-1, keepdims=True)))
    g_pre = g_pre.astype(jnp.bfloat16)
    weight_sum = jnp.stack([lax.dot_general(piece, g_pre, (((0,), (0,)), ((), ())), preferred_element_type=jnp.float32) for piece in shifted])
    g_in = g_out
    for offset in range(3):
        moved = g_pre if offset == 0 else shift_future(g_pre, offset * dilation)
        g_in = g_in + lax.dot_general(moved, weight[offset], (((1,), (1,)), ((), ())), preferred_element_type=jnp.float32)
    return (g_in.astype(jnp.bfloat16), weight_sum, gain_sum, bias_sum)

def reference(inputs, kernel_weight_first, norm_gain_first, norm_bias_first, kernel_weight_second, norm_gain_second, norm_bias_second, cotangent):

    def one_user(pair):
        source_rows, upstream_gradient = pair
        delayed_first, normalized_first, inverse_deviation_first, activation_first = residual_layer_forward(source_rows, kernel_weight_first, norm_gain_first, norm_bias_first, DILATION_FIRST1)
        hidden_state = (source_rows.astype(jnp.float32) + activate(activation_first)).astype(jnp.bfloat16)
        delayed_second, normalized_second, inverse_deviation_second, activation_second = residual_layer_forward(hidden_state, kernel_weight_second, norm_gain_second, norm_bias_second, DILATION_SECOND2)
        gradient_hidden, weight_total_second, gain_total_second, bias_total_second = residual_layer_backward(upstream_gradient.astype(jnp.float32), delayed_second, normalized_second, inverse_deviation_second, activation_second, kernel_weight_second, norm_gain_second, DILATION_SECOND2)
        gradient_input_rows, weight_total_first, gain_total_first, bias_total_first = residual_layer_backward(gradient_hidden.astype(jnp.float32), delayed_first, normalized_first, inverse_deviation_first, activation_first, kernel_weight_first, norm_gain_first, DILATION_FIRST1)
        return (gradient_input_rows, weight_total_first, gain_total_first, bias_total_first, weight_total_second, gain_total_second, bias_total_second)
    results = lax.map(one_user, (inputs, cotangent))
    grad_scale = 1.0 / jnp.sqrt(jnp.float32(USERS * SEQ))
    return (results[0], lax.optimization_barrier(jnp.sum(results[1], axis=0)) * grad_scale, lax.optimization_barrier(jnp.sum(results[2], axis=0)) * grad_scale, lax.optimization_barrier(jnp.sum(results[3], axis=0)) * grad_scale, lax.optimization_barrier(jnp.sum(results[4], axis=0)) * grad_scale, lax.optimization_barrier(jnp.sum(results[5], axis=0)) * grad_scale, lax.optimization_barrier(jnp.sum(results[6], axis=0)) * grad_scale)
```

```python
import functools

import jax
import jax.numpy as jnp
from jax import lax
from jax.experimental import pallas as pl
from jax.experimental.pallas import tpu as pltpu
from jax.sharding import PartitionSpec as P

DILATION_FIRST1 = 1024
DILATION_SECOND2 = 2048
EPSILON = 1e-05
GROUP = 8
MESH = pl.DeviceIdType.MESH
F32 = jnp.float32
BF16 = jnp.bfloat16


def dot(a, b):
    return jnp.dot(a, b, preferred_element_type=F32)


def mean_c(values):
    return jnp.mean(values, axis=-1, keepdims=True)


def kernel(
    M, G, U, R, scale,
    x_ref, ct_ref, w1_ref, w2_ref, gain1, bias1, gain2, bias2,
    out_ref, dw_ref, dg1, db1, dg2, db2,
    xe, cte, he, g2e, g1e, xt, ht, w1, w2, w1t, w2t,
    n1, i1, s1, n2, i2, s2, gh, ov,
    part, core_in, shard, r1, r2, r3, final,
    loc_sem, xs, xr, cs, cr, os_, or_, hs, hr, ps, pr, gs, gr, us, ur, zs, zr, as_, ar, bs, br,
):
    C = x_ref.shape[1]
    NT = M // 2
    T = 2 * R
    KC = 3 * C
    SH = KC // G
    s, u = lax.axis_index("seq"), lax.axis_index("user")
    g, m = s // M, s % M
    core = m % 2
    z = m // 2

    def member(p):
        return {"seq": g * M + p, "user": u}

    def group(p):
        return {"seq": p * M + m, "user": u}

    def user(p):
        return {"seq": s, "user": p}

    def remote(src, dst, ss, rs, device):
        return pltpu.make_async_remote_copy(
            src_ref=src, dst_ref=dst, send_sem=ss, recv_sem=rs, device_id=device, device_id_type=MESH
        )

    def rows(start, size):
        return pl.ds(pl.multiple_of(start, R), size)

    barrier = pltpu.get_barrier_semaphore()
    for j in range(1, M):
        pl.semaphore_signal(barrier, inc=1, device_id=member((m + j) % M), device_id_type=MESH)
    for j in range(1, G):
        pl.semaphore_signal(barrier, inc=1, device_id=group((g + j) % G), device_id_type=MESH)
    for j in range(1, U):
        pl.semaphore_signal(barrier, inc=1, device_id=user((u + j) % U), device_id_type=MESH)

    own = rows(m * R, R)
    local = [
        pltpu.make_async_copy(w1_ref, w1, loc_sem.at[0]),
        pltpu.make_async_copy(w2_ref, w2, loc_sem.at[1]),
        pltpu.make_async_copy(x_ref.at[own], xe.at[rows((2 + m) * R, R)], loc_sem.at[2]),
        pltpu.make_async_copy(ct_ref.at[own], cte.at[rows(m * R, R)], loc_sem.at[3]),
    ]
    for copy in local:
        copy.start()

    pl.semaphore_wait(barrier, M + G + U - 3)

    order = [M // 2, M // 2 + 1] + [j for j in range(M - 1, 0, -1) if j not in (M // 2, M // 2 + 1)]

    def x_copy(j):
        p = (m + j) % M
        return remote(x_ref.at[rows(p * R, R)], xe.at[rows((2 + m) * R, R)], xs.at[j], xr.at[j], member(p))

    def ct_copy(j):
        p = (m + j) % M
        return remote(ct_ref.at[rows(p * R, R)], cte.at[rows(m * R, R)], cs.at[j], cr.at[j], member(p))

    for j in order:
        x_copy(j).start()

    @pl.when(g == 0)
    def _():
        xe[0 : 2 * R] = jnp.zeros((2 * R, C), BF16)
        he[0 : 4 * R] = jnp.zeros((4 * R, C), BF16)

    @pl.when(g == G - 1)
    def _():
        g2e[M * R : (M + 4) * R] = jnp.zeros((4 * R, C), BF16)
        g1e[M * R : (M + 2) * R] = jnp.zeros((2 * R, C), BF16)

    later, earlier = group((g + 1) % G), group((g + G - 1) % G)
    x_halo = remote(xe.at[M * R : (M + 2) * R], xe.at[0 : 2 * R], hs.at[0], hr.at[0], later)
    h_halo = remote(he.at[M * R : (M + 4) * R], he.at[0 : 4 * R], hs.at[1], hr.at[1], later)
    g2_halo = remote(g2e.at[0 : 4 * R], g2e.at[M * R : (M + 4) * R], hs.at[2], hr.at[2], earlier)
    g1_halo = remote(g1e.at[0 : 2 * R], g1e.at[M * R : (M + 2) * R], hs.at[3], hr.at[3], earlier)

    def start_if(cond, copy):
        @pl.when(cond)
        def _():
            copy.start()

    def recv_if(cond, copy):
        @pl.when(cond)
        def _():
            copy.wait_recv()

    def send_done_if(cond, copy):
        @pl.when(cond)
        def _():
            copy.wait_send()

    for copy in local:
        copy.wait()
    for k in range(3):
        w1t[k] = w1[k].T
        w2t[k] = w2[k].T

    for j in range(1, M):
        x_copy(j).wait()
    start_if(g < G - 1, x_halo)
    for j in order:
        ct_copy(j).start()

    ga1, be1, ga2, be2 = gain1[...], bias1[...], gain2[...], bias2[...]

    def layer_one(n, _):
        i = NT - 1 - n
        at = i * T
        recv_if((i == 0) & (g > 0), x_halo)
        here = xe[rows(at + 2 * R, T)]
        pre = dot(here, w1[0]) + dot(xe[rows(at + R, T)], w1[1]) + dot(xe[rows(at, T)], w1[2])
        away = pre - mean_c(pre)
        inverse = lax.rsqrt(mean_c(away * away) + EPSILON)
        normed = away * inverse
        active = normed * ga1 + be1
        sigma = 0.5 * jnp.tanh(0.5 * active) + 0.5
        he[rows(at + 4 * R, T)] = (here.astype(F32) + active * sigma).astype(BF16)
        mine = rows(at, T)
        n1[mine] = normed
        i1[mine] = jnp.broadcast_to(inverse, (T, 128))
        s1[mine] = sigma * (1.0 + active * (1.0 - sigma))
        start_if((i == NT - 2) & (g < G - 1), h_halo)
        return 0

    lax.fori_loop(0, NT, layer_one, 0)

    def layer_two(n, _):
        i = NT - 1 - n
        at = i * T
        recv_if((i == 1) & (g > 0), h_halo)
        pre = (
            dot(he[rows(at + 4 * R, T)], w2[0])
            + dot(he[rows(at + 2 * R, T)], w2[1])
            + dot(he[rows(at, T)], w2[2])
        )
        away = pre - mean_c(pre)
        inverse = lax.rsqrt(mean_c(away * away) + EPSILON)
        normed = away * inverse
        active = normed * ga2 + be2
        sigma = 0.5 * jnp.tanh(0.5 * active) + 0.5
        mine = rows(at, T)
        n2[mine] = normed
        i2[mine] = jnp.broadcast_to(inverse, (T, 128))
        s2[mine] = sigma * (1.0 + active * (1.0 - sigma))
        return 0

    lax.fori_loop(0, NT, layer_two, 0)

    def turn_h(i, _):
        ht[:, pl.ds(pl.multiple_of(i * T, 128), T)] = he[rows(i * T, T)].T
        return 0

    def turn_x(i, _):
        xt[:, pl.ds(pl.multiple_of(i * T, 128), T)] = xe[rows(i * T, T)].T
        return 0

    lax.fori_loop(0, NT + 2, turn_h, 0)
    lax.fori_loop(0, NT + 1, turn_x, 0)

    for j in range(1, M):
        ct_copy(j).wait()

    def norm_backward(grad, slope, normed, inverse, gain):
        g_act = grad * slope
        weighted = g_act * normed
        sums = (jnp.sum(weighted, axis=0, keepdims=True), jnp.sum(g_act, axis=0, keepdims=True))
        g_norm = g_act * gain
        g_pre = inverse * (g_norm - mean_c(g_norm) - normed * mean_c(weighted * gain))
        return g_pre.astype(BF16), sums

    zero = jnp.zeros((1, C), F32)

    def back_two(i, sums):
        mine = rows(i * T, T)
        g_pre, more = norm_backward(cte[mine].astype(F32), s2[mine], n2[mine], i2[mine][:, 0:1], ga2)
        g2e[mine] = g_pre
        start_if((i == 1) & (g > 0), g2_halo)
        return (sums[0] + more[0], sums[1] + more[1])

    gain_sum_two, bias_sum_two = lax.fori_loop(0, NT, back_two, (zero, zero))

    for k in range(3):
        part[1, k * C : (k + 1) * C] = dot(ht[:, (4 - 2 * k) * R : (4 - 2 * k + M) * R], g2e[0 : M * R])

    def back_one(i, sums):
        at = i * T
        recv_if((i == NT - 2) & (g < G - 1), g2_halo)
        mine = rows(at, T)
        total = (
            cte[mine].astype(F32)
            + dot(g2e[mine], w2t[0])
            + dot(g2e[rows(at + 2 * R, T)], w2t[1])
            + dot(g2e[rows(at + 4 * R, T)], w2t[2])
        )
        g_hidden = total.astype(BF16)
        gh[mine] = g_hidden
        g_pre, more = norm_backward(g_hidden.astype(F32), s1[mine], n1[mine], i1[mine][:, 0:1], ga1)
        g1e[mine] = g_pre
        start_if((i == 0) & (g > 0), g1_halo)
        return (sums[0] + more[0], sums[1] + more[1])

    gain_sum_one, bias_sum_one = lax.fori_loop(0, NT, back_one, (zero, zero))

    for k in range(3):
        part[0, k * C : (k + 1) * C] = dot(xt[:, (2 - k) * R : (2 - k + M) * R], g1e[0 : M * R])
    small = jnp.concatenate(
        [gain_sum_one, bias_sum_one, gain_sum_two, bias_sum_two, jnp.zeros((4, C), F32)], axis=0
    )
    part[0, KC : KC + 8] = small
    part[1, KC : KC + 8] = small

    core_copy = remote(part.at[1 - core], core_in, bs.at[0], br.at[0], member(z * 2 + 1 - core))
    core_copy.start()

    def out_copy(b):
        j = (b - m + M) % M
        return remote(ov.at[rows(b * R, R)], out_ref.at[own], os_.at[j], or_.at[j], member(b))

    own_out = pltpu.make_async_copy(ov.at[own], out_ref.at[own], os_.at[0])

    def send_out(b):
        start_if(b == m, own_out)
        start_if(b != m, out_copy(b))

    def grad_input(i, _):
        at = i * T
        recv_if((i == NT - 1) & (g < G - 1), g1_halo)
        mine = rows(at, T)
        total = (
            gh[mine].astype(F32)
            + dot(g1e[mine], w1t[0])
            + dot(g1e[rows(at + R, T)], w1t[1])
            + dot(g1e[rows(at + 2 * R, T)], w1t[2])
        )
        ov[mine] = total.astype(BF16)
        send_out(2 * i)
        send_out(2 * i + 1)
        return 0

    lax.fori_loop(0, NT, grad_input, 0)

    core_copy.wait()
    tail = part[core, KC : KC + 8] + core_in[KC : KC + 8]

    def fold(j, _):
        at = pl.ds(pl.multiple_of(j * SH, 8), SH)
        shard[j, 0:SH] = part[core, at] + core_in[at]
        shard[j, SH : SH + 8] = tail
        return 0

    lax.fori_loop(0, G, fold, 0)

    def sum_copy(j):
        p = (g + j) % G
        return remote(shard.at[p], r1.at[g], gs.at[j], gr.at[j], group(p))

    for j in range(1, G):
        sum_copy(j).start()
    r1[g] = shard[g]
    for j in range(1, G):
        sum_copy(j).wait()
    total = r1[0]
    for j in range(1, G):
        total = total + r1[j]

    def user_copy(j):
        return remote(r2.at[u], r2.at[u], us.at[j], ur.at[j], user((u + j) % U))

    r2[u] = total
    for j in range(1, U):
        user_copy(j).start()
    for j in range(1, U):
        user_copy(j).wait()
    total = r2[0]
    for j in range(1, U):
        total = total + r2[j]

    def z_copy(j):
        return remote(r3.at[z], r3.at[z], zs.at[j], zr.at[j], member((m + 2 * j) % M))

    r3[z] = total
    for j in range(1, M // 2):
        z_copy(j).start()
    for j in range(1, M // 2):
        z_copy(j).wait()
    total = r3[0]
    for j in range(1, M // 2):
        total = total + r3[j]
    total = total * scale
    final[...] = total[0:SH]
    for k, ref in enumerate((dg1, db1, dg2, db2)):
        ref[...] = total[SH + k : SH + k + 1]

    place = pl.ds(pl.multiple_of(core * KC + g * SH, 8), SH)

    def gather_copy(j):
        return remote(final, dw_ref.at[place], as_.at[j], ar.at[j], group((g + j) % G))

    own_sum = pltpu.make_async_copy(final, dw_ref.at[place], as_.at[0])
    own_sum.start()
    for j in range(1, G):
        gather_copy(j).start()
    own_sum.wait()
    for j in range(1, G):
        gather_copy(j).wait()
    layer = pl.ds(pl.multiple_of(core * KC, 8), KC)
    last_copy = remote(dw_ref.at[layer], dw_ref.at[layer], bs.at[1], br.at[1], member(z * 2 + 1 - core))
    last_copy.start()

    own_out.wait()
    for j in range(1, M):
        out_copy((m + j) % M).wait()
    send_done_if(g < G - 1, x_halo)
    send_done_if(g < G - 1, h_halo)
    send_done_if(g > 0, g2_halo)
    send_done_if(g > 0, g1_halo)
    last_copy.wait()


def shards(M, G, U, *args):
    inputs, first, gain1, bias1, second, gain2, bias2, cotangent = args
    _, length, C = inputs.shape
    R = length // M
    KC = 3 * C
    SH = KC // G
    N = length
    scale = float((length * M * G * U) ** -0.5)
    vmem, anyw = pl.BlockSpec(memory_space=pltpu.VMEM), pl.BlockSpec(memory_space=pl.ANY)
    vec = jax.ShapeDtypeStruct((1, C), F32)
    dma = pltpu.SemaphoreType.DMA
    out = pl.pallas_call(
        functools.partial(kernel, M, G, U, R, scale),
        out_shape=(
            jax.ShapeDtypeStruct((N, C), BF16),
            jax.ShapeDtypeStruct((2 * KC, C), F32),
            vec, vec, vec, vec,
        ),
        in_specs=[anyw] * 4 + [vmem] * 4,
        out_specs=(anyw, anyw, vmem, vmem, vmem, vmem),
        scratch_shapes=[
            pltpu.VMEM(((M + 2) * R, C), BF16),
            pltpu.VMEM((N, C), BF16),
            pltpu.VMEM(((M + 4) * R, C), BF16),
            pltpu.VMEM(((M + 4) * R, C), BF16),
            pltpu.VMEM(((M + 2) * R, C), BF16),
            pltpu.VMEM((C, (M + 2) * R), BF16),
            pltpu.VMEM((C, (M + 4) * R), BF16),
            *[pltpu.VMEM((3, C, C), BF16)] * 4,
            *[pltpu.VMEM((N, C), F32), pltpu.VMEM((N, 128), F32), pltpu.VMEM((N, C), F32)] * 2,
            *[pltpu.VMEM((N, C), BF16)] * 2,
            pltpu.VMEM((2, KC + 8, C), F32),
            pltpu.VMEM((KC + 8, C), F32),
            pltpu.VMEM((G, SH + 8, C), F32),
            pltpu.VMEM((G, SH + 8, C), F32),
            pltpu.VMEM((U, SH + 8, C), F32),
            pltpu.VMEM((M // 2, SH + 8, C), F32),
            pltpu.VMEM((SH, C), F32),
            dma((4,)),
            dma((M,)), dma((M,)),
            dma((M,)), dma((M,)),
            dma((M,)), dma((M,)),
            dma((4,)), dma((4,)),
            dma((1,)), dma((1,)),
            dma((G,)), dma((G,)),
            dma((U,)), dma((U,)),
            dma((M // 2,)), dma((M // 2,)),
            dma((G,)), dma((G,)),
            dma((2,)), dma((2,)),
        ],
        compiler_params=pltpu.CompilerParams(
            collective_id=0, has_side_effects=True, vmem_limit_bytes=40 * 2**20
        ),
    )(
        inputs.reshape(N, C), cotangent.reshape(N, C), first, second,
        *[v.reshape(1, C) for v in (gain1, bias1, gain2, bias2)],
    )
    grad, dw, dg1, db1, dg2, db2 = out
    dw = dw.reshape(2, 3, C, C)
    flat = [v.reshape(C) for v in (dg1, db1, dg2, db2)]
    return (grad.reshape(inputs.shape), dw[0], flat[0], flat[1], dw[1], flat[2], flat[3])


def solution(mesh):
    seq, users = mesh.shape["seq"], mesh.shape["user"]
    M = min(GROUP, seq)
    placed = (P("user", "seq", None), P(), P(), P(), P(), P(), P(), P("user", "seq", None))
    return jax.shard_map(
        functools.partial(shards, M, seq // M, users),
        mesh=mesh,
        in_specs=placed,
        out_specs=(P("user", "seq", None), P(), P(), P(), P(), P(), P()),
        check_vma=False,
    )
```

```python
import functools

import jax
import jax.numpy as jnp
from jax import lax
from jax.experimental import pallas as pl
from jax.experimental.pallas import tpu as pltpu
from jax.sharding import PartitionSpec as P

EPSILON = 1e-05
GROUP = 8
MESH = pl.DeviceIdType.MESH
F32 = jnp.float32
BF16 = jnp.bfloat16


def dot(a, b):
    return jnp.dot(a, b, preferred_element_type=F32)


def mean_c(values):
    return jnp.mean(values, axis=-1, keepdims=True)


PAIRS = 19


def kernel(
    M, G, U, R, QS, scale,
    x_ref, ct_ref, w1_ref, w2_ref, gain1_ref, bias1_ref, gain2_ref, bias2_ref,
    out_ref, dw_ref, small_ref,
    *scratch,
):
    pairs = [scratch[2 * k : 2 * k + 2] for k in range(PAIRS)]
    (xe, cte, he, g2e, g1e, xt0, xt1, xt2, ht0, ht1, ht2, n1, i1, s1, n2, i2, s2, gh, ov) = pairs
    xt, ht = (xt0, xt1, xt2), (ht0, ht1, ht2)
    (
        w1, w2, w1t, w2t, vecs,
        part, partb, small, small_all, core_in, shard, r1, piece, r2, r4, final,
        loc_sem, xs, xr, cs, cr, os_, or_, hs, hr, gs, gr, us, ur, zs, zr, as_, ar, bs, br,
    ) = scratch[2 * PAIRS :]
    C = x_ref.shape[1]
    NT = M // 4
    KC = 3 * C
    SR = 2 * KC // G
    PR = SR // U
    s, u = lax.axis_index("seq"), lax.axis_index("user")
    g, m = s // M, s % M
    core = m % 2
    z = m // 2

    def member(p):
        return {"seq": g * M + p, "user": u}

    def group(p):
        return {"seq": p * M + m, "user": u}

    def user(p):
        return {"seq": s, "user": p}

    H = M // 2
    Z = U * H
    column = u * H + z

    def on_z(p):
        return {"seq": g * M + 2 * (p % H) + core, "user": p // H}

    def remote(src, dst, ss, rs, device):
        return pltpu.make_async_remote_copy(
            src_ref=src, dst_ref=dst, send_sem=ss, recv_sem=rs, device_id=device, device_id_type=MESH
        )

    def rows(start, size):
        return pl.ds(pl.multiple_of(start, 16), size)

    barrier = pltpu.get_barrier_semaphore()
    far = [M // 2, M // 2 + 1]
    order = far + [j for j in range(M - 1, 0, -1) if j not in far]
    for j in order:
        pl.semaphore_signal(barrier, inc=1, device_id=member((m + j) % M), device_id_type=MESH)
    for j in range(1, G):
        pl.semaphore_signal(barrier, inc=1, device_id=group((g + j) % G), device_id_type=MESH)
    for j in range(1, Z):
        p = (column + j) % Z
        pl.when(p // H != u)(
            functools.partial(pl.semaphore_signal, barrier, inc=1, device_id=on_z(p), device_id_type=MESH)
        )

    def part_rows(p, a):
        return rows(p * R + (0, QS[0])[a], QS[a])

    local = [
        pltpu.make_async_copy(w1_ref, w1, loc_sem.at[0]),
        pltpu.make_async_copy(w2_ref, w2, loc_sem.at[1]),
    ]
    for k, ref in enumerate((gain1_ref, bias1_ref, gain2_ref, bias2_ref)):
        local.append(pltpu.make_async_copy(ref, vecs.at[k], loc_sem.at[2 + k]))
    for a in range(2):
        local.append(
            pltpu.make_async_copy(x_ref.at[part_rows(m, a)], xe[a].at[rows((2 + m) * QS[a], QS[a])], loc_sem.at[6 + a])
        )
        local.append(
            pltpu.make_async_copy(ct_ref.at[part_rows(m, a)], cte[a].at[rows(m * QS[a], QS[a])], loc_sem.at[8 + a])
        )
    for copy in local:
        copy.start()

    def x_copy(a, j):
        p = (m + j) % M
        return remote(x_ref.at[part_rows(p, a)], xe[a].at[rows((2 + m) * QS[a], QS[a])], xs.at[a, j], xr.at[a, j], member(p))

    def ct_copy(a, j):
        p = (m + j) % M
        return remote(ct_ref.at[part_rows(p, a)], cte[a].at[rows(m * QS[a], QS[a])], cs.at[a, j], cr.at[a, j], member(p))

    pl.semaphore_wait(barrier, M + G - 2 + Z - H)
    for copy in (x_copy, ct_copy):
        for a in range(2):
            for j in order:
                copy(a, j).start()

    def clear(buf, start, n):
        for a in range(2):
            buf[a][start * QS[a] : (start + n) * QS[a]] = jnp.zeros((n * QS[a], C), BF16)

    @pl.when(g == 0)
    def _():
        clear(xe, 0, 2)
        clear(he, 0, 4)

    @pl.when(g == G - 1)
    def _():
        clear(g2e, M, 4)
        clear(g1e, M, 2)

    later, earlier = group((g + 1) % G), group((g + G - 1) % G)

    def halo(buf, a, k, forward):
        n, Q = (4 if k in (1, 2) else 2), QS[a]
        head, tail = buf[a].at[0 : n * Q], buf[a].at[M * Q : (M + n) * Q]
        if forward:
            return remote(tail, head, hs.at[a, k], hr.at[a, k], later)
        return remote(head, tail, hs.at[a, k], hr.at[a, k], earlier)

    x_halo = [halo(xe, a, 0, True) for a in range(2)]
    h_halo = [halo(he, a, 1, True) for a in range(2)]
    g2_halo = [halo(g2e, a, 2, False) for a in range(2)]
    g1_halo = [halo(g1e, a, 3, False) for a in range(2)]
    not_first, not_last = g > 0, g < G - 1

    def start_if(cond, copy):
        pl.when(cond)(copy.start)

    def recv_if(cond, copy):
        pl.when(cond)(copy.wait_recv)

    for copy in local:
        copy.wait()
    for k in range(3):
        w1t[k] = w1[k].T
        w2t[k] = w2[k].T
    ga1, be1, ga2, be2 = vecs[0], vecs[1], vecs[2], vecs[3]

    def normalize(pre, gain, bias, a, mine, normed_ref, inverse_ref, slope_ref):
        away = pre - mean_c(pre)
        inverse = lax.rsqrt(mean_c(away * away) + EPSILON)
        normed = away * inverse
        active = normed * gain + bias
        sigma = 0.5 * jnp.tanh(0.5 * active) + 0.5
        normed_ref[a][mine] = normed
        inverse_ref[a][mine] = jnp.broadcast_to(inverse, (inverse.shape[0], 128))
        slope_ref[a][mine] = sigma * (1.0 + active * (1.0 - sigma))
        return active * sigma

    def tile(a, i, blocks=0):
        return pl.ds((4 * i + blocks) * QS[a], 4 * QS[a])

    def layer_one(a, i):
        here = xe[a][tile(a, i, 2)]
        pre = dot(here, w1[0]) + dot(xe[a][tile(a, i, 1)], w1[1]) + dot(xe[a][tile(a, i)], w1[2])
        gated = normalize(pre, ga1, be1, a, tile(a, i), n1, i1, s1)
        he[a][tile(a, i, 4)] = (here.astype(F32) + gated).astype(BF16)

    def layer_two(a, i):
        pre = dot(he[a][tile(a, i, 4)], w2[0]) + dot(he[a][tile(a, i, 2)], w2[1]) + dot(he[a][tile(a, i)], w2[2])
        normalize(pre, ga2, be2, a, tile(a, i), n2, i2, s2)

    for a in range(2):
        for j in range(1, M):
            x_copy(a, j).wait()
        start_if(not_last, x_halo[a])
        for i in range(NT - 1, -1, -1):
            if i == 0:
                recv_if(not_first, x_halo[a])
            layer_one(a, i)
            if i == NT - 1:
                start_if(not_last, h_halo[a])
    for a in range(2):
        for i in range(NT - 1, -1, -1):
            if i == 0:
                recv_if(not_first, h_halo[a])
            layer_two(a, i)
    for a in range(2):
        for k in range(3):
            ht[k][a][...] = he[a][pl.ds((4 - 2 * k) * QS[a], M * QS[a])].T
            xt[k][a][...] = xe[a][pl.ds((2 - k) * QS[a], M * QS[a])].T

    def norm_backward(grad, slope, normed, inverse, gain):
        g_act = grad * slope
        weighted = g_act * normed
        sums = (jnp.sum(weighted, axis=0, keepdims=True), jnp.sum(g_act, axis=0, keepdims=True))
        g_norm = g_act * gain
        g_pre = inverse * (g_norm - mean_c(g_norm) - normed * mean_c(weighted * gain))
        return g_pre.astype(BF16), sums

    def back_two(a, i):
        mine = tile(a, i)
        g_pre, sums = norm_backward(cte[a][mine].astype(F32), s2[a][mine], n2[a][mine], i2[a][mine, 0:1], ga2)
        g2e[a][mine] = g_pre
        return sums

    def back_one(a, i):
        mine = tile(a, i)
        total = (
            cte[a][mine].astype(F32)
            + dot(g2e[a][mine], w2t[0])
            + dot(g2e[a][tile(a, i, 2)], w2t[1])
            + dot(g2e[a][tile(a, i, 4)], w2t[2])
        )
        g_hidden = total.astype(BF16)
        gh[a][mine] = g_hidden
        g_pre, sums = norm_backward(g_hidden.astype(F32), s1[a][mine], n1[a][mine], i1[a][mine, 0:1], ga1)
        g1e[a][mine] = g_pre
        return sums

    def grad_input(a, i):
        mine = tile(a, i)
        total = (
            gh[a][mine].astype(F32)
            + dot(g1e[a][mine], w1t[0])
            + dot(g1e[a][tile(a, i, 1)], w1t[1])
            + dot(g1e[a][tile(a, i, 2)], w1t[2])
        )
        ov[a][mine] = total.astype(BF16)

    def weights(l, a):
        grads = (g1e, g2e)[l][a][0 : M * QS[a]]
        for k in range(3):
            at = pl.ds(k * C, C)
            total = dot((xt, ht)[l][k][a][...], grads)
            if a == 0:
                part[l, at] = total
            else:
                total = part[l, at] + total
                part[l, at] = total
                partb[l, at] = total.astype(BF16)

    def add(sums, more):
        return more if sums is None else (sums[0] + more[0], sums[1] + more[1])

    def out_copy(a, j):
        b = (m + j) % M
        return remote(ov[a].at[rows(b * QS[a], QS[a])], out_ref.at[part_rows(m, a)], os_.at[a, j], or_.at[a, j], member(b))

    def own_out(a):
        return pltpu.make_async_copy(ov[a].at[rows(m * QS[a], QS[a])], out_ref.at[part_rows(m, a)], os_.at[a, 0])

    def send_out(a):
        for j in order:
            out_copy(a, j).start()
        own_out(a).start()

    other = member(z * 2 + 1 - core)
    core_copy = remote(partb.at[1 - core], core_in, bs.at[0], br.at[0], other)

    def shard_copy(j):
        return remote(shard.at[(g + j) % G], r1.at[g], gs.at[0], gr.at[0], group((g + j) % G))

    all_shards = remote(r1.at[0 : G - 1], r1.at[0 : G - 1], gs.at[0], gr.at[0], other)

    def piece_copy(j):
        p = (column + j) % Z
        return remote(piece.at[p // H], r2.at[column], zs.at[0], zr.at[0], on_z(p))

    all_pieces = remote(r2.at[0 : Z - 1], r2.at[0 : Z - 1], zs.at[0], zr.at[0], other)

    def back_copy(j):
        return remote(r4.at[u], r4.at[u], us.at[j], ur.at[j], user((u + j) % U))

    place = dw_ref.at[rows(core * KC + (g // 2) * SR, SR), pl.ds(pl.multiple_of((g % 2) * 128, 128), 128)]

    def gather_copy(j):
        return remote(final, place, as_.at[0], ar.at[0], group((g + j) % G))

    all_gathered = remote(r1.at[0 : G - 1, 0:SR], r1.at[0 : G - 1, 0:SR], as_.at[0], ar.at[0], other)
    own_gather = pltpu.make_async_copy(final, place, bs.at[3])
    layer = dw_ref.at[rows(core * KC, KC)]
    last_copy = remote(layer, layer, bs.at[1], br.at[1], other)
    small_copy = remote(small_all.at[core], small_all.at[core], bs.at[2], br.at[2], other)

    def split(value):
        high = value.astype(BF16)
        return jnp.concatenate([high, (value - high.astype(F32)).astype(BF16)], axis=0)

    def joined(total):
        half = total.shape[0] // 2
        return total[:half] + total[half:]

    def pack_small(l, sums):
        value = jnp.concatenate(
            [v[:, at : at + 128] for v in sums for at in (0, 128)] + [jnp.zeros((4, 128), F32)], axis=0
        )
        small[l] = value
        partb[l, KC : KC + 16, 0:128] = split(value)

    def fold():
        core_copy.wait_recv()
        both = split(small[core] + joined(core_in[KC : KC + 16, 0:128].astype(F32)))
        for j in range(G):
            at, lanes = slice((j // 2) * SR, (j // 2 + 1) * SR), slice((j % 2) * 128, (j % 2 + 1) * 128)
            total = part[core, at, lanes] + core_in[at, lanes].astype(F32)
            shard[j, 0:SR] = total.astype(BF16)
            shard[j, SR : SR + 16] = both
        for j in range(1, G):
            shard_copy(j).start()
        r1[g] = shard[g]

    def added(ref, n):
        total = ref[0].astype(F32)
        for j in range(1, n):
            total = total + ref[j].astype(F32)
        return total

    def packed(total, value):
        high = value.astype(BF16).astype(F32)
        return jnp.concatenate([total, high, value - high], axis=0).astype(BF16)

    def over_z():
        all_shards.wait_recv()
        total = added(r1, G)
        value = joined(total[SR : SR + 16])[0:4]
        for j in range(U):
            piece[j] = packed(total[j * PR : (j + 1) * PR], value)
        for j in range(1, Z):
            piece_copy(j).start()
        r2[column] = piece[u]

    def back_to_users():
        all_pieces.wait_recv()
        total = added(r2, Z) * scale
        r4[u] = total.astype(BF16)
        for j in range(1, U):
            back_copy(j).start()
        small_all[core] = joined(total[PR : PR + 8])
        small_copy.start()

    def gather():
        for j in range(1, U):
            back_copy(j).wait_recv()
        final[...] = jnp.concatenate([r4[j].astype(F32)[0:PR] for j in range(U)], axis=0).astype(BF16)
        for j in range(1, G):
            gather_copy(j).start()
        own_gather.start()

    def last():
        own_gather.wait()
        all_gathered.wait_recv()
        last_copy.start()

    def sent():
        core_copy.wait_send()
        all_shards.wait_send()
        all_pieces.wait_send()
        for j in range(1, U):
            back_copy(j).wait_send()
        all_gathered.wait_send()

    sums_one = sums_two = None
    for a in range(2):
        for j in range(1, M):
            ct_copy(a, j).wait()
        for i in range(NT):
            sums_two = add(sums_two, back_two(a, i))
            if i == 0:
                start_if(not_first, g2_halo[a])
        if a == 1:
            pack_small(1, sums_two)
        weights(1, a)
        if a == 1:
            start_if(core == 0, core_copy)
        for i in range(NT):
            if i == NT - 1:
                if a == 1:
                    recv_if(not_last, g1_halo[0])
                    for k in range(NT):
                        grad_input(0, k)
                    send_out(0)
                    pl.when(core == 1)(fold)
                recv_if(not_last, g2_halo[a])
            sums_one = add(sums_one, back_one(a, i))
            if i == 0:
                start_if(not_first, g1_halo[a])
        if a == 1:
            pack_small(0, sums_one)
        weights(0, a)
    start_if(core == 1, core_copy)
    for i in range(NT - 1):
        grad_input(1, i)
    pl.when(core == 0)(fold)
    recv_if(not_last, g1_halo[1])
    grad_input(1, NT - 1)
    over_z()
    send_out(1)
    back_to_users()
    gather()
    last()
    small_copy.wait()
    for l in range(2):
        for k in range(2):
            small_ref[2 * l + k : 2 * l + k + 1] = jnp.concatenate(
                [small_all[l, 2 * k : 2 * k + 1], small_all[l, 2 * k + 1 : 2 * k + 2]], axis=1
            )

    for a in range(2):
        own_out(a).wait()
        for j in range(1, M):
            out_copy(a, j).wait()
        pl.when(not_last)(x_halo[a].wait_send)
        pl.when(not_last)(h_halo[a].wait_send)
        pl.when(not_first)(g2_halo[a].wait_send)
        pl.when(not_first)(g1_halo[a].wait_send)
    sent()
    last_copy.wait()


def shards(M, G, U, *args):
    inputs, first, gain1, bias1, second, gain2, bias2, cotangent = args
    _, N, C = inputs.shape
    R = N // M
    QS = (R - R // 4, R // 4)
    KC = 3 * C
    SR = 2 * KC // G
    PR = SR // U
    scale = float((N * M * G * U) ** -0.5)
    vmem, anyw = pl.BlockSpec(memory_space=pltpu.VMEM), pl.BlockSpec(memory_space=pl.ANY)
    dma = pltpu.SemaphoreType.DMA
    V = pltpu.VMEM

    def both(shape_of):
        return [shape_of(q) for q in QS]

    out = pl.pallas_call(
        functools.partial(kernel, M, G, U, R, QS, scale),
        out_shape=(
            jax.ShapeDtypeStruct((N, C), BF16),
            jax.ShapeDtypeStruct((2 * KC, C), BF16),
            jax.ShapeDtypeStruct((8, C), F32),
        ),
        in_specs=[anyw] * 8,
        out_specs=(anyw, anyw, vmem),
        scratch_shapes=[
            *both(lambda q: V(((M + 2) * q, C), BF16)),
            *both(lambda q: V((M * q, C), BF16)),
            *both(lambda q: V(((M + 4) * q, C), BF16)),
            *both(lambda q: V(((M + 4) * q, C), BF16)),
            *both(lambda q: V(((M + 2) * q, C), BF16)),
            *both(lambda q: V((C, M * q), BF16)) * 6,
            *(
                both(lambda q: V((M * q, C), F32))
                + both(lambda q: V((M * q, 128), F32))
                + both(lambda q: V((M * q, C), F32))
            )
            * 2,
            *both(lambda q: V((M * q, C), BF16)) * 2,
            *[V((3, C, C), BF16)] * 4,
            V((4, 1, C), F32),
            V((2, KC, C), F32),
            V((2, KC + 16, C), BF16),
            V((2, 8, 128), F32),
            V((2, 4, 128), F32),
            V((KC + 16, C), BF16),
            V((G, SR + 16, 128), BF16),
            V((G, SR + 16, 128), BF16),
            V((U, PR + 8, 128), BF16),
            V((U * M // 2, PR + 8, 128), BF16),
            V((U, PR + 8, 128), BF16),
            V((SR, 128), BF16),
            dma((10,)),
            dma((2, M)), dma((2, M)),
            dma((2, M)), dma((2, M)),
            dma((2, M)), dma((2, M)),
            dma((2, 4)), dma((2, 4)),
            dma((1,)), dma((1,)),
            dma((U,)), dma((U,)),
            dma((1,)), dma((1,)),
            dma((1,)), dma((1,)),
            dma((4,)), dma((3,)),
        ],
        compiler_params=pltpu.CompilerParams(
            collective_id=0, has_side_effects=True, vmem_limit_bytes=56 * 2**20
        ),
    )(
        inputs.reshape(N, C), cotangent.reshape(N, C), first, second,
        *[v.reshape(1, C) for v in (gain1, bias1, gain2, bias2)],
    )
    grad, dw, small = out
    dw = dw.reshape(2, 3, C, C).astype(F32)
    return (grad.reshape(inputs.shape), dw[0], small[0], small[1], dw[1], small[2], small[3])


def solution(mesh):
    seq, users = mesh.shape["seq"], mesh.shape["user"]
    M = min(GROUP, seq)
    placed = (P("user", "seq", None), P(), P(), P(), P(), P(), P(), P("user", "seq", None))
    return jax.shard_map(
        functools.partial(shards, M, seq // M, users),
        mesh=mesh,
        in_specs=placed,
        out_specs=(P("user", "seq", None), P(), P(), P(), P(), P(), P()),
        check_vma=False,
    )
```

```python
import functools

import jax
import jax.numpy as jnp
from jax import lax
from jax.experimental import pallas as pl
from jax.experimental.pallas import tpu as pltpu
from jax.sharding import PartitionSpec as P

EPSILON = 1e-05
GROUP = 8
MESH = pl.DeviceIdType.MESH
F32 = jnp.float32
BF16 = jnp.bfloat16


def dot(a, b):
    return jnp.dot(a, b, preferred_element_type=F32)


def mean_c(values):
    return jnp.mean(values, axis=-1, keepdims=True)


PAIRS = 19


def kernel(
    M, G, U, R, QS, scale,
    x_ref, ct_ref, w1_ref, w2_ref, gain1_ref, bias1_ref, gain2_ref, bias2_ref,
    out_ref, dw_ref, small_ref,
    *scratch,
):
    pairs = [scratch[2 * k : 2 * k + 2] for k in range(PAIRS)]
    (xe, cte, he, g2e, g1e, xt0, xt1, xt2, ht0, ht1, ht2, n1, i1, s1, n2, i2, s2, gh, ov) = pairs
    xt, ht = (xt0, xt1, xt2), (ht0, ht1, ht2)
    (
        w1, w2, w1t, w2t, vecs,
        part, partb, small, small_all, core_in, shard, r1, piece, r2, r4, final,
        loc_sem, xs, xr, cs, cr, os_, or_, hs, hr, gs, gr, us, ur, zs, zr, as_, ar, bs, br,
    ) = scratch[2 * PAIRS :]
    C = x_ref.shape[1]
    NT = M // 4
    KC = 3 * C
    SR = 2 * KC // G
    PR = SR // U
    s, u = lax.axis_index("seq"), lax.axis_index("user")
    g, m = s // M, s % M
    core = m % 2
    z = m // 2

    def member(p):
        return {"seq": g * M + p, "user": u}

    def group(p):
        return {"seq": p * M + m, "user": u}

    def user(p):
        return {"seq": s, "user": p}

    H = M // 2
    Z = U * H
    column = u * H + z

    def on_z(p):
        return {"seq": g * M + 2 * (p % H) + core, "user": p // H}

    def remote(src, dst, ss, rs, device):
        return pltpu.make_async_remote_copy(
            src_ref=src, dst_ref=dst, send_sem=ss, recv_sem=rs, device_id=device, device_id_type=MESH
        )

    def rows(start, size):
        return pl.ds(pl.multiple_of(start, 16), size)

    g_order = sorted(range(1, G), key=lambda j: -(min(j % 4, 4 - j % 4) + min(j // 4, 4 - j // 4)))
    z_order = sorted(range(1, Z), key=lambda j: -min(j % H, H - j % H))

    barrier = pltpu.get_barrier_semaphore()
    far = [M // 2, M // 2 + 1]
    order = far + [j for j in range(M - 1, 0, -1) if j not in far]
    for j in order:
        pl.semaphore_signal(barrier, inc=1, device_id=member((m + j) % M), device_id_type=MESH)
    for j in z_order:
        p = (column + j) % Z
        pl.when(p // H != u)(
            functools.partial(pl.semaphore_signal, barrier, inc=1, device_id=on_z(p), device_id_type=MESH)
        )

    for j in g_order:
        pl.semaphore_signal(barrier, inc=1, device_id=group((g + j) % G), device_id_type=MESH)

    def part_rows(p, a):
        return rows(p * R + (0, QS[0])[a], QS[a])

    local = [
        pltpu.make_async_copy(w1_ref, w1, loc_sem.at[0]),
        pltpu.make_async_copy(w2_ref, w2, loc_sem.at[1]),
    ]
    for k, ref in enumerate((gain1_ref, bias1_ref, gain2_ref, bias2_ref)):
        local.append(pltpu.make_async_copy(ref, vecs.at[k], loc_sem.at[2 + k]))
    for a in range(2):
        local.append(
            pltpu.make_async_copy(x_ref.at[part_rows(m, a)], xe[a].at[rows((2 + m) * QS[a], QS[a])], loc_sem.at[6 + a])
        )
        local.append(
            pltpu.make_async_copy(ct_ref.at[part_rows(m, a)], cte[a].at[rows(m * QS[a], QS[a])], loc_sem.at[8 + a])
        )
    for copy in local:
        copy.start()

    def x_copy(a, j):
        p = (m + j) % M
        return remote(x_ref.at[part_rows(p, a)], xe[a].at[rows((2 + m) * QS[a], QS[a])], xs.at[a, j], xr.at[a, j], member(p))

    def ct_copy(a, j):
        p = (m + j) % M
        return remote(ct_ref.at[part_rows(p, a)], cte[a].at[rows(m * QS[a], QS[a])], cs.at[a, j], cr.at[a, j], member(p))

    pl.semaphore_wait(barrier, M + G - 2 + Z - H)
    for copy in (x_copy, ct_copy):
        for a in range(2):
            for j in order:
                copy(a, j).start()

    def clear(buf, start, n):
        for a in range(2):
            buf[a][start * QS[a] : (start + n) * QS[a]] = jnp.zeros((n * QS[a], C), BF16)

    @pl.when(g == 0)
    def _():
        clear(xe, 0, 2)
        clear(he, 0, 4)

    @pl.when(g == G - 1)
    def _():
        clear(g2e, M, 4)
        clear(g1e, M, 2)

    later, earlier = group((g + 1) % G), group((g + G - 1) % G)

    def halo(buf, a, k, forward):
        n, Q = (4 if k in (1, 2) else 2), QS[a]
        head, tail = buf[a].at[0 : n * Q], buf[a].at[M * Q : (M + n) * Q]
        if forward:
            return remote(tail, head, hs.at[a, k], hr.at[a, k], later)
        return remote(head, tail, hs.at[a, k], hr.at[a, k], earlier)

    x_halo = [halo(xe, a, 0, True) for a in range(2)]
    h_halo = [halo(he, a, 1, True) for a in range(2)]
    g2_halo = [halo(g2e, a, 2, False) for a in range(2)]
    g1_halo = [halo(g1e, a, 3, False) for a in range(2)]
    not_first, not_last = g > 0, g < G - 1

    def start_if(cond, copy):
        pl.when(cond)(copy.start)

    def recv_if(cond, copy):
        pl.when(cond)(copy.wait_recv)

    for copy in local:
        copy.wait()
    for k in range(3):
        w1t[k] = w1[k].T
        w2t[k] = w2[k].T
    ga1, be1, ga2, be2 = vecs[0], vecs[1], vecs[2], vecs[3]

    def normalize(pre, gain, bias, a, mine, normed_ref, inverse_ref, slope_ref):
        away = pre - mean_c(pre)
        inverse = lax.rsqrt(mean_c(away * away) + EPSILON)
        normed = away * inverse
        active = normed * gain + bias
        sigma = 0.5 * jnp.tanh(0.5 * active) + 0.5
        normed_ref[a][mine] = normed
        inverse_ref[a][mine] = jnp.broadcast_to(inverse, (inverse.shape[0], 128))
        slope_ref[a][mine] = sigma * (1.0 + active * (1.0 - sigma))
        return active * sigma

    def tile(a, i, blocks=0):
        return pl.ds((4 * i + blocks) * QS[a], 4 * QS[a])

    def layer_one(a, i):
        here = xe[a][tile(a, i, 2)]
        pre = dot(here, w1[0]) + dot(xe[a][tile(a, i, 1)], w1[1]) + dot(xe[a][tile(a, i)], w1[2])
        gated = normalize(pre, ga1, be1, a, tile(a, i), n1, i1, s1)
        he[a][tile(a, i, 4)] = (here.astype(F32) + gated).astype(BF16)

    def layer_two(a, i):
        pre = dot(he[a][tile(a, i, 4)], w2[0]) + dot(he[a][tile(a, i, 2)], w2[1]) + dot(he[a][tile(a, i)], w2[2])
        normalize(pre, ga2, be2, a, tile(a, i), n2, i2, s2)

    for a in range(2):
        for j in range(1, M):
            x_copy(a, j).wait()
        start_if(not_last, x_halo[a])
        for i in range(NT - 1, -1, -1):
            if i == 0:
                recv_if(not_first, x_halo[a])
            layer_one(a, i)
            if i == NT - 1:
                start_if(not_last, h_halo[a])
    for a in range(2):
        for i in range(NT - 1, -1, -1):
            if i == 0:
                recv_if(not_first, h_halo[a])
            layer_two(a, i)
    for a in range(2):
        for k in range(3):
            ht[k][a][...] = he[a][pl.ds((4 - 2 * k) * QS[a], M * QS[a])].T
            xt[k][a][...] = xe[a][pl.ds((2 - k) * QS[a], M * QS[a])].T

    def norm_backward(grad, slope, normed, inverse, gain):
        g_act = grad * slope
        weighted = g_act * normed
        sums = (jnp.sum(weighted, axis=0, keepdims=True), jnp.sum(g_act, axis=0, keepdims=True))
        g_norm = g_act * gain
        g_pre = inverse * (g_norm - mean_c(g_norm) - normed * mean_c(weighted * gain))
        return g_pre.astype(BF16), sums

    def back_two(a, i):
        mine = tile(a, i)
        g_pre, sums = norm_backward(cte[a][mine].astype(F32), s2[a][mine], n2[a][mine], i2[a][mine, 0:1], ga2)
        g2e[a][mine] = g_pre
        return sums

    def back_one(a, i):
        mine = tile(a, i)
        total = (
            cte[a][mine].astype(F32)
            + dot(g2e[a][mine], w2t[0])
            + dot(g2e[a][tile(a, i, 2)], w2t[1])
            + dot(g2e[a][tile(a, i, 4)], w2t[2])
        )
        g_hidden = total.astype(BF16)
        gh[a][mine] = g_hidden
        g_pre, sums = norm_backward(g_hidden.astype(F32), s1[a][mine], n1[a][mine], i1[a][mine, 0:1], ga1)
        g1e[a][mine] = g_pre
        return sums

    def grad_input(a, i):
        mine = tile(a, i)
        total = (
            gh[a][mine].astype(F32)
            + dot(g1e[a][mine], w1t[0])
            + dot(g1e[a][tile(a, i, 1)], w1t[1])
            + dot(g1e[a][tile(a, i, 2)], w1t[2])
        )
        ov[a][mine] = total.astype(BF16)

    def weights(l, a):
        grads = (g1e, g2e)[l][a][0 : M * QS[a]]
        for k in range(3):
            at = pl.ds(k * C, C)
            total = dot((xt, ht)[l][k][a][...], grads)
            if a == 0:
                part[l, at] = total
            else:
                total = part[l, at] + total
                part[l, at] = total
                partb[l, at] = total.astype(BF16)

    def add(sums, more):
        return more if sums is None else (sums[0] + more[0], sums[1] + more[1])

    def out_copy(a, j):
        b = (m + j) % M
        return remote(ov[a].at[rows(b * QS[a], QS[a])], out_ref.at[part_rows(m, a)], os_.at[a, j], or_.at[a, j], member(b))

    def own_out(a):
        return pltpu.make_async_copy(ov[a].at[rows(m * QS[a], QS[a])], out_ref.at[part_rows(m, a)], os_.at[a, 0])

    def send_out(a):
        for j in order:
            out_copy(a, j).start()
        own_out(a).start()

    other = member(z * 2 + 1 - core)
    core_copy = remote(partb.at[1 - core], core_in, bs.at[0], br.at[0], other)

    def shard_copy(j):
        return remote(shard.at[(g + j) % G], r1.at[g], gs.at[0], gr.at[0], group((g + j) % G))

    all_shards = remote(r1.at[0 : G - 1], r1.at[0 : G - 1], gs.at[0], gr.at[0], other)

    def piece_copy(j):
        p = (column + j) % Z
        return remote(piece.at[p // H], r2.at[column], zs.at[0], zr.at[0], on_z(p))

    all_pieces = remote(r2.at[0 : Z - 1], r2.at[0 : Z - 1], zs.at[0], zr.at[0], other)

    def back_copy(j):
        return remote(r4.at[u], r4.at[u], us.at[j], ur.at[j], user((u + j) % U))

    place = dw_ref.at[rows(core * KC + (g // 2) * SR, SR), pl.ds(pl.multiple_of((g % 2) * 128, 128), 128)]

    def gather_copy(j):
        return remote(final, place, as_.at[0], ar.at[0], group((g + j) % G))

    all_gathered = remote(r1.at[0 : G - 1, 0:SR], r1.at[0 : G - 1, 0:SR], as_.at[0], ar.at[0], other)
    own_gather = pltpu.make_async_copy(final, place, bs.at[3])
    layer = dw_ref.at[rows(core * KC, KC)]
    last_copy = remote(layer, layer, bs.at[1], br.at[1], other)
    small_copy = remote(small_all.at[core], small_all.at[core], bs.at[2], br.at[2], other)

    def split(value):
        high = value.astype(BF16)
        return jnp.concatenate([high, (value - high.astype(F32)).astype(BF16)], axis=0)

    def joined(total):
        half = total.shape[0] // 2
        return total[:half] + total[half:]

    def pack_small(l, sums):
        value = jnp.concatenate(
            [v[:, at : at + 128] for v in sums for at in (0, 128)] + [jnp.zeros((4, 128), F32)], axis=0
        )
        small[l] = value
        partb[l, KC : KC + 16, 0:128] = split(value)

    def fold():
        core_copy.wait_recv()
        both = split(small[core] + joined(core_in[KC : KC + 16, 0:128].astype(F32)))
        for j in range(G):
            at, lanes = slice((j // 2) * SR, (j // 2 + 1) * SR), slice((j % 2) * 128, (j % 2 + 1) * 128)
            total = part[core, at, lanes] + core_in[at, lanes].astype(F32)
            shard[j, 0:SR] = total.astype(BF16)
            shard[j, SR : SR + 16] = both
        for j in g_order:
            shard_copy(j).start()
        r1[g] = shard[g]

    def added(ref, n):
        total = ref[0].astype(F32)
        for j in range(1, n):
            total = total + ref[j].astype(F32)
        return total

    def packed(total, value):
        high = value.astype(BF16).astype(F32)
        return jnp.concatenate([total, high, value - high], axis=0).astype(BF16)

    def over_z():
        all_shards.wait_recv()
        total = added(r1, G)
        value = joined(total[SR : SR + 16])[0:4]
        for j in range(U):
            piece[j] = packed(total[j * PR : (j + 1) * PR], value)
        for j in z_order:
            piece_copy(j).start()
        r2[column] = piece[u]

    def back_to_users():
        all_pieces.wait_recv()
        total = added(r2, Z) * scale
        r4[u] = total.astype(BF16)
        for j in range(1, U):
            back_copy(j).start()
        small_all[core] = joined(total[PR : PR + 8])
        small_copy.start()

    def gather():
        for j in range(1, U):
            back_copy(j).wait_recv()
        final[...] = jnp.concatenate([r4[j].astype(F32)[0:PR] for j in range(U)], axis=0).astype(BF16)
        for j in g_order:
            gather_copy(j).start()
        own_gather.start()

    def last():
        own_gather.wait()
        all_gathered.wait_recv()
        last_copy.start()

    def sent():
        core_copy.wait_send()
        all_shards.wait_send()
        all_pieces.wait_send()
        for j in range(1, U):
            back_copy(j).wait_send()
        all_gathered.wait_send()

    sums_one = sums_two = None
    for a in range(2):
        for j in range(1, M):
            ct_copy(a, j).wait()
        for i in range(NT):
            sums_two = add(sums_two, back_two(a, i))
            if i == 0:
                start_if(not_first, g2_halo[a])
        if a == 1:
            pack_small(1, sums_two)
        weights(1, a)
        if a == 1:
            start_if(core == 0, core_copy)
        for i in range(NT):
            if i == NT - 1:
                if a == 1:
                    recv_if(not_last, g1_halo[0])
                    for k in range(NT):
                        grad_input(0, k)
                    send_out(0)
                recv_if(not_last, g2_halo[a])
            sums_one = add(sums_one, back_one(a, i))
            if i == 0:
                start_if(not_first, g1_halo[a])
        if a == 1:
            pack_small(0, sums_one)
        weights(0, a)
    start_if(core == 1, core_copy)
    for i in range(NT - 1):
        grad_input(1, i)
    fold()
    recv_if(not_last, g1_halo[1])
    grad_input(1, NT - 1)
    over_z()
    send_out(1)
    back_to_users()
    gather()
    last()
    small_copy.wait()
    for l in range(2):
        for k in range(2):
            small_ref[2 * l + k : 2 * l + k + 1] = jnp.concatenate(
                [small_all[l, 2 * k : 2 * k + 1], small_all[l, 2 * k + 1 : 2 * k + 2]], axis=1
            )

    for a in range(2):
        own_out(a).wait()
        for j in range(1, M):
            out_copy(a, j).wait()
        pl.when(not_last)(x_halo[a].wait_send)
        pl.when(not_last)(h_halo[a].wait_send)
        pl.when(not_first)(g2_halo[a].wait_send)
        pl.when(not_first)(g1_halo[a].wait_send)
    sent()
    last_copy.wait()


def shards(M, G, U, *args):
    inputs, first, gain1, bias1, second, gain2, bias2, cotangent = args
    _, N, C = inputs.shape
    R = N // M
    QS = (R - R // 4, R // 4)
    KC = 3 * C
    SR = 2 * KC // G
    PR = SR // U
    scale = float((N * M * G * U) ** -0.5)
    vmem, anyw = pl.BlockSpec(memory_space=pltpu.VMEM), pl.BlockSpec(memory_space=pl.ANY)
    dma = pltpu.SemaphoreType.DMA
    V = pltpu.VMEM

    def both(shape_of):
        return [shape_of(q) for q in QS]

    out = pl.pallas_call(
        functools.partial(kernel, M, G, U, R, QS, scale),
        out_shape=(
            jax.ShapeDtypeStruct((N, C), BF16),
            jax.ShapeDtypeStruct((2 * KC, C), BF16),
            jax.ShapeDtypeStruct((8, C), F32),
        ),
        in_specs=[anyw] * 8,
        out_specs=(anyw, anyw, vmem),
        scratch_shapes=[
            *both(lambda q: V(((M + 2) * q, C), BF16)),
            *both(lambda q: V((M * q, C), BF16)),
            *both(lambda q: V(((M + 4) * q, C), BF16)),
            *both(lambda q: V(((M + 4) * q, C), BF16)),
            *both(lambda q: V(((M + 2) * q, C), BF16)),
            *both(lambda q: V((C, M * q), BF16)) * 6,
            *(
                both(lambda q: V((M * q, C), F32))
                + both(lambda q: V((M * q, 128), F32))
                + both(lambda q: V((M * q, C), F32))
            )
            * 2,
            *both(lambda q: V((M * q, C), BF16)) * 2,
            *[V((3, C, C), BF16)] * 4,
            V((4, 1, C), F32),
            V((2, KC, C), F32),
            V((2, KC + 16, C), BF16),
            V((2, 8, 128), F32),
            V((2, 4, 128), F32),
            V((KC + 16, C), BF16),
            V((G, SR + 16, 128), BF16),
            V((G, SR + 16, 128), BF16),
            V((U, PR + 8, 128), BF16),
            V((U * M // 2, PR + 8, 128), BF16),
            V((U, PR + 8, 128), BF16),
            V((SR, 128), BF16),
            dma((10,)),
            dma((2, M)), dma((2, M)),
            dma((2, M)), dma((2, M)),
            dma((2, M)), dma((2, M)),
            dma((2, 4)), dma((2, 4)),
            dma((1,)), dma((1,)),
            dma((U,)), dma((U,)),
            dma((1,)), dma((1,)),
            dma((1,)), dma((1,)),
            dma((4,)), dma((3,)),
        ],
        compiler_params=pltpu.CompilerParams(
            collective_id=0, has_side_effects=True, vmem_limit_bytes=56 * 2**20
        ),
    )(
        inputs.reshape(N, C), cotangent.reshape(N, C), first, second,
        *[v.reshape(1, C) for v in (gain1, bias1, gain2, bias2)],
    )
    grad, dw, small = out
    dw = dw.reshape(2, 3, C, C).astype(F32)
    return (grad.reshape(inputs.shape), dw[0], small[0], small[1], dw[1], small[2], small[3])


def solution(mesh):
    seq, users = mesh.shape["seq"], mesh.shape["user"]
    M = min(GROUP, seq)
    placed = (P("user", "seq", None), P(), P(), P(), P(), P(), P(), P("user", "seq", None))
    return jax.shard_map(
        functools.partial(shards, M, seq // M, users),
        mesh=mesh,
        in_specs=placed,
        out_specs=(P("user", "seq", None), P(), P(), P(), P(), P(), P()),
        check_vma=False,
    )
```

```python
import functools

import jax
import jax.numpy as jnp
from jax import lax
from jax.experimental import pallas as pl
from jax.experimental.pallas import tpu as pltpu
from jax.sharding import PartitionSpec as P

EPSILON = 1e-05
GROUP = 8
MESH = pl.DeviceIdType.MESH
F32 = jnp.float32
BF16 = jnp.bfloat16


def dot(a, b):
    return jnp.dot(a, b, preferred_element_type=F32)


def mean_c(values):
    return jnp.mean(values, axis=-1, keepdims=True)


PAIRS = 19


def kernel(
    M, G, U, R, QS, scale,
    x_ref, ct_ref, w1_ref, w2_ref, gain1_ref, bias1_ref, gain2_ref, bias2_ref,
    out_ref, dw_ref, small_ref,
    *scratch,
):
    pairs = [scratch[2 * k : 2 * k + 2] for k in range(PAIRS)]
    (xe, cte, he, g2e, g1e, xt0, xt1, xt2, ht0, ht1, ht2, n1, i1, s1, n2, i2, s2, gh, ov) = pairs
    xt, ht = (xt0, xt1, xt2), (ht0, ht1, ht2)
    (
        w1, w2, w1t, w2t, vecs,
        part, partb, small, small_all, core_in, shard, r1, piece, r2, r4, final,
        loc_sem, xs, xr, cs, cr, os_, or_, hs, hr, gs, gr, us, ur, zs, zr, as_, ar, bs, br,
    ) = scratch[2 * PAIRS :]
    C = x_ref.shape[1]
    NT = M // 4
    KC = 3 * C
    SR = 2 * KC // G
    PR = SR // U
    s, u = lax.axis_index("seq"), lax.axis_index("user")
    g, m = s // M, s % M
    core = m % 2
    z = m // 2

    def member(p):
        return {"seq": g * M + p, "user": u}

    def group(p):
        return {"seq": p * M + m, "user": u}

    def user(p):
        return {"seq": s, "user": p}

    H = M // 2
    Z = U * H
    column = u * H + z

    def on_z(p):
        return {"seq": g * M + 2 * (p % H) + core, "user": p // H}

    def remote(src, dst, ss, rs, device):
        return pltpu.make_async_remote_copy(
            src_ref=src, dst_ref=dst, send_sem=ss, recv_sem=rs, device_id=device, device_id_type=MESH
        )

    def rows(start, size):
        return pl.ds(pl.multiple_of(start, 16), size)

    g_order = sorted(range(1, G), key=lambda j: -(min(j % 4, 4 - j % 4) + min(j // 4, 4 - j // 4)))
    z_order = sorted(range(1, Z), key=lambda j: -min(j % H, H - j % H))

    barrier = pltpu.get_barrier_semaphore()
    far = [M // 2, M // 2 + 1]
    order = far + [j for j in range(M - 1, 0, -1) if j not in far]
    for j in order:
        pl.semaphore_signal(barrier, inc=1, device_id=member((m + j) % M), device_id_type=MESH)
    for j in z_order:
        p = (column + j) % Z
        pl.when(p // H != u)(
            functools.partial(pl.semaphore_signal, barrier, inc=1, device_id=on_z(p), device_id_type=MESH)
        )

    for j in g_order:
        pl.semaphore_signal(barrier, inc=1, device_id=group((g + j) % G), device_id_type=MESH)

    def part_rows(p, a):
        return rows(p * R + (0, QS[0])[a], QS[a])

    local = [
        pltpu.make_async_copy(w1_ref, w1, loc_sem.at[0]),
        pltpu.make_async_copy(w2_ref, w2, loc_sem.at[1]),
    ]
    for k, ref in enumerate((gain1_ref, bias1_ref, gain2_ref, bias2_ref)):
        local.append(pltpu.make_async_copy(ref, vecs.at[k], loc_sem.at[2 + k]))
    for a in range(2):
        local.append(
            pltpu.make_async_copy(x_ref.at[part_rows(m, a)], xe[a].at[rows((2 + m) * QS[a], QS[a])], loc_sem.at[6 + a])
        )
        local.append(
            pltpu.make_async_copy(ct_ref.at[part_rows(m, a)], cte[a].at[rows(m * QS[a], QS[a])], loc_sem.at[8 + a])
        )
    for copy in local:
        copy.start()

    def x_copy(a, j):
        p = (m + j) % M
        return remote(x_ref.at[part_rows(p, a)], xe[a].at[rows((2 + m) * QS[a], QS[a])], xs.at[a, j], xr.at[a, j], member(p))

    def ct_copy(a, j):
        p = (m + j) % M
        return remote(ct_ref.at[part_rows(p, a)], cte[a].at[rows(m * QS[a], QS[a])], cs.at[a, j], cr.at[a, j], member(p))

    pl.semaphore_wait(barrier, M + G - 2 + Z - H)
    for copy in (x_copy, ct_copy):
        for a in range(2):
            for j in order:
                copy(a, j).start()

    def clear(buf, start, n):
        for a in range(2):
            buf[a][start * QS[a] : (start + n) * QS[a]] = jnp.zeros((n * QS[a], C), BF16)

    @pl.when(g == 0)
    def _():
        clear(xe, 0, 2)
        clear(he, 0, 4)

    @pl.when(g == G - 1)
    def _():
        clear(g2e, M, 4)
        clear(g1e, M, 2)

    later, earlier = group((g + 1) % G), group((g + G - 1) % G)

    def halo(buf, a, k, forward):
        n, Q = (4 if k in (1, 2) else 2), QS[a]
        head, tail = buf[a].at[0 : n * Q], buf[a].at[M * Q : (M + n) * Q]
        if forward:
            return remote(tail, head, hs.at[a, k], hr.at[a, k], later)
        return remote(head, tail, hs.at[a, k], hr.at[a, k], earlier)

    x_halo = [halo(xe, a, 0, True) for a in range(2)]
    h_halo = [halo(he, a, 1, True) for a in range(2)]
    g2_halo = [halo(g2e, a, 2, False) for a in range(2)]
    g1_halo = [halo(g1e, a, 3, False) for a in range(2)]
    not_first, not_last = g > 0, g < G - 1

    def start_if(cond, copy):
        pl.when(cond)(copy.start)

    def recv_if(cond, copy):
        pl.when(cond)(copy.wait_recv)

    for copy in local:
        copy.wait()
    for k in range(3):
        w1t[k] = w1[k].T
        w2t[k] = w2[k].T
    ga1, be1, ga2, be2 = vecs[0], vecs[1], vecs[2], vecs[3]

    def normalize(pre, gain, bias, a, mine, normed_ref, inverse_ref, slope_ref):
        away = pre - mean_c(pre)
        inverse = lax.rsqrt(mean_c(away * away) + EPSILON)
        normed = away * inverse
        active = normed * gain + bias
        sigma = 0.5 * jnp.tanh(0.5 * active) + 0.5
        normed_ref[a][mine] = normed
        inverse_ref[a][mine] = jnp.broadcast_to(inverse, (inverse.shape[0], 128))
        slope_ref[a][mine] = sigma * (1.0 + active * (1.0 - sigma))
        return active * sigma

    def tile(a, i, blocks=0):
        return pl.ds((4 * i + blocks) * QS[a], 4 * QS[a])

    def layer_one(a, i):
        here = xe[a][tile(a, i, 2)]
        pre = dot(here, w1[0]) + dot(xe[a][tile(a, i, 1)], w1[1]) + dot(xe[a][tile(a, i)], w1[2])
        gated = normalize(pre, ga1, be1, a, tile(a, i), n1, i1, s1)
        he[a][tile(a, i, 4)] = (here.astype(F32) + gated).astype(BF16)

    def layer_two(a, i):
        pre = dot(he[a][tile(a, i, 4)], w2[0]) + dot(he[a][tile(a, i, 2)], w2[1]) + dot(he[a][tile(a, i)], w2[2])
        normalize(pre, ga2, be2, a, tile(a, i), n2, i2, s2)

    for a in range(2):
        for j in range(1, M):
            x_copy(a, j).wait()
        start_if(not_last, x_halo[a])
        for i in range(NT - 1, -1, -1):
            if i == 0:
                recv_if(not_first, x_halo[a])
            layer_one(a, i)
            if i == NT - 1:
                start_if(not_last, h_halo[a])
    for a in range(2):
        for i in range(NT - 1, -1, -1):
            if i == 0:
                recv_if(not_first, h_halo[a])
            layer_two(a, i)
    for a in range(2):
        for k in range(3):
            ht[k][a][...] = he[a][pl.ds((4 - 2 * k) * QS[a], M * QS[a])].T
            xt[k][a][...] = xe[a][pl.ds((2 - k) * QS[a], M * QS[a])].T

    def norm_backward(grad, slope, normed, inverse, gain):
        g_act = grad * slope
        weighted = g_act * normed
        sums = (jnp.sum(weighted, axis=0, keepdims=True), jnp.sum(g_act, axis=0, keepdims=True))
        g_norm = g_act * gain
        g_pre = inverse * (g_norm - mean_c(g_norm) - normed * mean_c(weighted * gain))
        return g_pre.astype(BF16), sums

    def back_two(a, i):
        mine = tile(a, i)
        g_pre, sums = norm_backward(cte[a][mine].astype(F32), s2[a][mine], n2[a][mine], i2[a][mine, 0:1], ga2)
        g2e[a][mine] = g_pre
        return sums

    def back_one(a, i):
        mine = tile(a, i)
        total = (
            cte[a][mine].astype(F32)
            + dot(g2e[a][mine], w2t[0])
            + dot(g2e[a][tile(a, i, 2)], w2t[1])
            + dot(g2e[a][tile(a, i, 4)], w2t[2])
        )
        g_hidden = total.astype(BF16)
        gh[a][mine] = g_hidden
        g_pre, sums = norm_backward(g_hidden.astype(F32), s1[a][mine], n1[a][mine], i1[a][mine, 0:1], ga1)
        g1e[a][mine] = g_pre
        return sums

    def grad_input(a, i):
        mine = tile(a, i)
        total = (
            gh[a][mine].astype(F32)
            + dot(g1e[a][mine], w1t[0])
            + dot(g1e[a][tile(a, i, 1)], w1t[1])
            + dot(g1e[a][tile(a, i, 2)], w1t[2])
        )
        ov[a][mine] = total.astype(BF16)

    def weights(l, a):
        grads = (g1e, g2e)[l][a][0 : M * QS[a]]
        for k in range(3):
            at = pl.ds(k * C, C)
            total = dot((xt, ht)[l][k][a][...], grads)
            if a == 0:
                part[l, at] = total
            else:
                total = part[l, at] + total
                part[l, at] = total
                partb[l, at] = total.astype(BF16)

    def add(sums, more):
        return more if sums is None else (sums[0] + more[0], sums[1] + more[1])

    def out_copy(a, j):
        b = (m + j) % M
        return remote(ov[a].at[rows(b * QS[a], QS[a])], out_ref.at[part_rows(m, a)], os_.at[a, j], or_.at[a, j], member(b))

    def own_out(a):
        return pltpu.make_async_copy(ov[a].at[rows(m * QS[a], QS[a])], out_ref.at[part_rows(m, a)], os_.at[a, 0])

    def send_out(a):
        for j in order:
            out_copy(a, j).start()
        own_out(a).start()

    other = member(z * 2 + 1 - core)
    core_copy = remote(partb.at[1 - core], core_in, bs.at[0], br.at[0], other)

    def shard_copy(j):
        return remote(shard.at[(g + j) % G], r1.at[g], gs.at[0], gr.at[0], group((g + j) % G))

    all_shards = remote(r1.at[0 : G - 1], r1.at[0 : G - 1], gs.at[0], gr.at[0], other)

    def piece_copy(j):
        p = (column + j) % Z
        return remote(piece.at[p // H], r2.at[column], zs.at[0], zr.at[0], on_z(p))

    all_pieces = remote(r2.at[0 : Z - 1], r2.at[0 : Z - 1], zs.at[0], zr.at[0], other)

    def back_copy(j):
        return remote(r4.at[u], r4.at[u], us.at[j], ur.at[j], user((u + j) % U))

    place = dw_ref.at[rows(core * KC + (g // 2) * SR, SR), pl.ds(pl.multiple_of((g % 2) * 128, 128), 128)]

    def gather_copy(j):
        return remote(final, place, as_.at[0], ar.at[0], group((g + j) % G))

    all_gathered = remote(r1.at[0 : G - 1, 0:SR], r1.at[0 : G - 1, 0:SR], as_.at[0], ar.at[0], other)
    own_gather = pltpu.make_async_copy(final, place, bs.at[3])
    layer = dw_ref.at[rows(core * KC, KC)]
    last_copy = remote(layer, layer, bs.at[1], br.at[1], other)
    small_copy = remote(small_all.at[core], small_all.at[core], bs.at[2], br.at[2], other)

    def split(value):
        high = value.astype(BF16)
        return jnp.concatenate([high, (value - high.astype(F32)).astype(BF16)], axis=0)

    def joined(total):
        half = total.shape[0] // 2
        return total[:half] + total[half:]

    def pack_small(l, sums):
        value = jnp.concatenate(
            [v[:, at : at + 128] for v in sums for at in (0, 128)] + [jnp.zeros((4, 128), F32)], axis=0
        )
        small[l] = value
        partb[l, KC : KC + 16, 0:128] = split(value)

    def fold():
        core_copy.wait_recv()
        both = split(small[core] + joined(core_in[KC : KC + 16, 0:128].astype(F32)))
        for j in range(G):
            at, lanes = slice((j // 2) * SR, (j // 2 + 1) * SR), slice((j % 2) * 128, (j % 2 + 1) * 128)
            total = part[core, at, lanes] + core_in[at, lanes].astype(F32)
            shard[j, 0:SR] = total.astype(BF16)
            shard[j, SR : SR + 16] = both
        for j in g_order:
            shard_copy(j).start()
        r1[g] = shard[g]

    def added(ref, n):
        total = ref[0].astype(F32)
        for j in range(1, n):
            total = total + ref[j].astype(F32)
        return total

    def packed(total, value):
        high = value.astype(BF16).astype(F32)
        return jnp.concatenate([total, high, value - high], axis=0).astype(BF16)

    def over_z():
        all_shards.wait_recv()
        total = added(r1, G)
        value = joined(total[SR : SR + 16])[0:4]
        for j in range(U):
            piece[j] = packed(total[j * PR : (j + 1) * PR], value)
        for j in z_order:
            piece_copy(j).start()
        r2[column] = piece[u]

    def back_to_users():
        all_pieces.wait_recv()
        total = added(r2, Z) * scale
        r4[u] = total.astype(BF16)
        for j in range(1, U):
            back_copy(j).start()
        small_all[core] = joined(total[PR : PR + 8])
        small_copy.start()

    def gather():
        for j in range(1, U):
            back_copy(j).wait_recv()
        final[...] = jnp.concatenate([r4[j].astype(F32)[0:PR] for j in range(U)], axis=0).astype(BF16)
        for j in g_order:
            gather_copy(j).start()
        own_gather.start()

    def last():
        own_gather.wait()
        all_gathered.wait_recv()
        last_copy.start()

    def sent():
        core_copy.wait_send()
        all_shards.wait_send()
        all_pieces.wait_send()
        for j in range(1, U):
            back_copy(j).wait_send()
        all_gathered.wait_send()

    sums_one = sums_two = None
    for a in range(2):
        for j in range(1, M):
            ct_copy(a, j).wait()
        for i in range(NT):
            sums_two = add(sums_two, back_two(a, i))
            if i == 0:
                start_if(not_first, g2_halo[a])
        if a == 1:
            pack_small(1, sums_two)
        weights(1, a)
        if a == 1:
            start_if(core == 0, core_copy)
        for i in range(NT):
            if i == NT - 1:
                if a == 1:
                    recv_if(not_last, g1_halo[0])
                    for k in range(NT):
                        grad_input(0, k)
                    send_out(0)
                recv_if(not_last, g2_halo[a])
            sums_one = add(sums_one, back_one(a, i))
            if i == 0:
                start_if(not_first, g1_halo[a])
        if a == 1:
            pack_small(0, sums_one)
        weights(0, a)
    start_if(core == 1, core_copy)
    for i in range(NT - 1):
        grad_input(1, i)
    fold()
    recv_if(not_last, g1_halo[1])
    grad_input(1, NT - 1)
    over_z()
    back_to_users()
    send_out(1)
    gather()
    last()
    small_copy.wait()
    for l in range(2):
        for k in range(2):
            small_ref[2 * l + k : 2 * l + k + 1] = jnp.concatenate(
                [small_all[l, 2 * k : 2 * k + 1], small_all[l, 2 * k + 1 : 2 * k + 2]], axis=1
            )

    for a in range(2):
        own_out(a).wait()
        for j in range(1, M):
            out_copy(a, j).wait()
        pl.when(not_last)(x_halo[a].wait_send)
        pl.when(not_last)(h_halo[a].wait_send)
        pl.when(not_first)(g2_halo[a].wait_send)
        pl.when(not_first)(g1_halo[a].wait_send)
    sent()
    last_copy.wait()


def shards(M, G, U, *args):
    inputs, first, gain1, bias1, second, gain2, bias2, cotangent = args
    _, N, C = inputs.shape
    R = N // M
    QS = (R - R // 4, R // 4)
    KC = 3 * C
    SR = 2 * KC // G
    PR = SR // U
    scale = float((N * M * G * U) ** -0.5)
    vmem, anyw = pl.BlockSpec(memory_space=pltpu.VMEM), pl.BlockSpec(memory_space=pl.ANY)
    dma = pltpu.SemaphoreType.DMA
    V = pltpu.VMEM

    def both(shape_of):
        return [shape_of(q) for q in QS]

    out = pl.pallas_call(
        functools.partial(kernel, M, G, U, R, QS, scale),
        out_shape=(
            jax.ShapeDtypeStruct((N, C), BF16),
            jax.ShapeDtypeStruct((2 * KC, C), BF16),
            jax.ShapeDtypeStruct((8, C), F32),
        ),
        in_specs=[anyw] * 8,
        out_specs=(anyw, anyw, vmem),
        scratch_shapes=[
            *both(lambda q: V(((M + 2) * q, C), BF16)),
            *both(lambda q: V((M * q, C), BF16)),
            *both(lambda q: V(((M + 4) * q, C), BF16)),
            *both(lambda q: V(((M + 4) * q, C), BF16)),
            *both(lambda q: V(((M + 2) * q, C), BF16)),
            *both(lambda q: V((C, M * q), BF16)) * 6,
            *(
                both(lambda q: V((M * q, C), F32))
                + both(lambda q: V((M * q, 128), F32))
                + both(lambda q: V((M * q, C), F32))
            )
            * 2,
            *both(lambda q: V((M * q, C), BF16)) * 2,
            *[V((3, C, C), BF16)] * 4,
            V((4, 1, C), F32),
            V((2, KC, C), F32),
            V((2, KC + 16, C), BF16),
            V((2, 8, 128), F32),
            V((2, 4, 128), F32),
            V((KC + 16, C), BF16),
            V((G, SR + 16, 128), BF16),
            V((G, SR + 16, 128), BF16),
            V((U, PR + 8, 128), BF16),
            V((U * M // 2, PR + 8, 128), BF16),
            V((U, PR + 8, 128), BF16),
            V((SR, 128), BF16),
            dma((10,)),
            dma((2, M)), dma((2, M)),
            dma((2, M)), dma((2, M)),
            dma((2, M)), dma((2, M)),
            dma((2, 4)), dma((2, 4)),
            dma((1,)), dma((1,)),
            dma((U,)), dma((U,)),
            dma((1,)), dma((1,)),
            dma((1,)), dma((1,)),
            dma((4,)), dma((3,)),
        ],
        compiler_params=pltpu.CompilerParams(
            collective_id=0, has_side_effects=True, vmem_limit_bytes=56 * 2**20
        ),
    )(
        inputs.reshape(N, C), cotangent.reshape(N, C), first, second,
        *[v.reshape(1, C) for v in (gain1, bias1, gain2, bias2)],
    )
    grad, dw, small = out
    dw = dw.reshape(2, 3, C, C).astype(F32)
    return (grad.reshape(inputs.shape), dw[0], small[0], small[1], dw[1], small[2], small[3])


def solution(mesh):
    seq, users = mesh.shape["seq"], mesh.shape["user"]
    M = min(GROUP, seq)
    placed = (P("user", "seq", None), P(), P(), P(), P(), P(), P(), P("user", "seq", None))
    return jax.shard_map(
        functools.partial(shards, M, seq // M, users),
        mesh=mesh,
        in_specs=placed,
        out_specs=(P("user", "seq", None), P(), P(), P(), P(), P(), P()),
        check_vma=False,
    )
```
